32 devices in a mesh: parts: 2 (over y), panel: 4 (over z), zone: 2 (over x), rhs: 2 (over core).
Axes of the slice: x: 2, y: 2, z: 4, core: 2. Of those that a mesh axis runs over, the one named last changes fastest.
Arguments:
- source: bfloat16 [4, 4096, 512], P(('parts', 'zone'), 'panel', 'rhs'), parts along dimension 0, may hold values from -6 to 6
- inverse: bfloat16 [4, 4096, 4096], P(('parts', 'zone'), 'panel'), parts along dimension 0, may hold values from -0.09375 to 0.09375
- coupling: bfloat16 [4, 4096, 4096], P(('parts', 'zone'), 'panel'), parts along dimension 0, may hold values from -0.078125 to 0.078125
Outputs:
- eliminated: bfloat16 [4, 4096, 512], P(('parts', 'zone'), 'panel', 'rhs'), parts along dimension 0
The draws below stay inside these ranges and needn't reach their ends.
There are 2 independent parts, one for each index of `parts`. The reference program is written for one: setup_inputs(seed, part) draws one part's arguments, and reference() takes and returns one part's arrays. A program takes and returns all parts, laid end to end along the dimension named above; each array names one. Nothing has to cross between parts.
All inputs are finite; a program needn't handle non-finite values.
Results may differ from the reference program's by a relative error of at most 0.013.
Values may be sent and summed in bfloat16 or wider, within the bound.
A program may use at most 64 MiB of HBM per device.

```python
import jax
import jax.numpy as jnp
from jax import lax

BLOCK = 4096
RHS = 512
ZONES = 2


def level_of(key, shape, cuts, least, top_value):
    factor_of = 1.0
    for dim, shards_of in cuts:
        heights = jax.random.uniform(jax.random.fold_in(jax.random.fold_in(key, 6), dim), (shards_of,), jnp.float32, least / len(cuts), top_value / len(cuts))
        factor_of = factor_of * jnp.repeat(jnp.exp(heights), shape[dim] // shards_of).reshape((-1,) + (1,) * (len(shape) - 1 - dim))
    return factor_of


def centred(stream_key, dims, scale, bound, shards=(), held_as=jnp.bfloat16):
    entries = jax.random.normal(stream_key, dims, jnp.float32) * scale
    if len(shards) > 0:
        entries = level_of(stream_key, dims, shards, -0.22, 0.18) * entries
    return jnp.clip(entries, min=-bound, max=bound).astype(held_as)


def setup_inputs(seed: int = 0, part: int = 0) -> dict:
    key_list = jax.random.split(jax.random.key(seed), 4)
    own_keys = jax.random.split(jax.random.fold_in(key_list[3], part), 4)
    return {
        "source": centred(own_keys[0], (ZONES, BLOCK, RHS), 1.0, 6.0, ((0, 2), (1, 4), (2, 2))),
        "inverse": centred(own_keys[1], (ZONES, BLOCK, BLOCK), BLOCK ** -0.5, 0.09375, ((0, 2), (1, 4))),
        "coupling": centred(own_keys[2], (ZONES, BLOCK, BLOCK), (BLOCK * 5 // 4) ** -0.5, 0.078125, ((0, 2), (1, 4))),
    }


def reference(source, inverse, coupling):
    def eliminate(previous, inputs):
        source_zone, inverse_zone, coupling_zone = inputs
        projected = jnp.dot(inverse_zone, source_zone, preferred_element_type=jnp.float32)
        combined = projected - jnp.dot(coupling_zone, previous, preferred_element_type=jnp.float32)
        rounded = combined.astype(jnp.bfloat16)
        return rounded, rounded

    initial = jnp.zeros((BLOCK, RHS), jnp.bfloat16)
    _, result = lax.scan(eliminate, initial, (source, inverse, coupling))
    return result
```

```python
import functools

import jax
import jax.numpy as jnp
from jax import lax
from jax.experimental import pallas as pl
from jax.experimental.pallas import tpu as pltpu
from jax.sharding import PartitionSpec as P

MESH = pl.DeviceIdType.MESH
RIGHT, LEFT = 0, 1
SOURCE_PIECES = 4
PIECES = 8
NEAR = 5


def kernel(
    panels, zones, source, inverse, coupling, out,
    inverse_v, coupling_v, rhs, previous, passing, total, mine,
    local_sem, rhs_send, rhs_recv, near_send, near_recv, far_send, far_recv, zone_send, zone_recv,
):
    panel, zone = lax.axis_index("panel"), lax.axis_index("zone")
    rows = mine.shape[0]
    tall, short = rows // SOURCE_PIECES, rows // PIECES
    tile = min(rows, 512)
    has_right, has_left = panel < panels - 1, panel > 0
    has_next, has_before = zone < zones - 1, zone > 0

    load_rhs = pltpu.make_async_copy(source.at[0], rhs.at[panel], local_sem.at[0])
    load_inverse = pltpu.make_async_copy(inverse.at[0], inverse_v, local_sem.at[1])
    load_coupling = pltpu.make_async_copy(coupling.at[0], coupling_v, local_sem.at[2])
    load_rhs.start()
    load_inverse.start()
    load_coupling.start()

    barrier = pltpu.get_barrier_semaphore()
    count = jnp.int32(0)
    for exists, axis, other in (
        (has_right, "panel", panel + 1),
        (has_left, "panel", panel - 1),
        (has_next, "zone", zone + 1),
        (has_before, "zone", zone - 1),
    ):
        @pl.when(exists)
        def _(axis=axis, other=other):
            pl.semaphore_signal(barrier, inc=1, device_id={axis: other}, device_id_type=MESH)

        count = count + exists.astype(jnp.int32)
    pl.semaphore_wait(barrier, count)

    def line(way, step, piece, from_ref, to_ref, send, recv):
        neighbour = panel + 1 if way == RIGHT else panel - 1
        return pltpu.make_async_remote_copy(
            src_ref=from_ref, dst_ref=to_ref,
            send_sem=send.at[way, step, piece], recv_sem=recv.at[way, step, piece],
            device_id={"panel": neighbour}, device_id_type=MESH,
        )

    def to_zone(block, piece, from_ref):
        return pltpu.make_async_remote_copy(
            src_ref=from_ref, dst_ref=previous.at[block, pl.ds(piece * short, short)],
            send_sem=zone_send.at[block, piece], recv_sem=zone_recv.at[block, piece],
            device_id={"zone": zone + 1}, device_id_type=MESH,
        )

    def ways(step):
        return (
            (RIGHT, panel - step, panel - step >= 0, has_right, has_left),
            (LEFT, panel + step, panel + step < panels, has_left, has_right),
        )

    def pass_on(step, pieces, own, place, send, recv, arrived=None):
        for piece in range(pieces):
            for way, block, exists, onward, _ in ways(step):
                @pl.when(exists)
                def _(piece=piece, way=way, block=block, onward=onward):
                    here = place(block, piece)
                    if step > 0:
                        line(way, step - 1, piece, here, here, send, recv).wait_recv()
                    if step < panels - 1:
                        @pl.when(onward)
                        def _():
                            start = own(piece) if step == 0 else here
                            line(way, step, piece, start, here, send, recv).start()
                    if step > 0 and arrived is not None:
                        arrived(block, piece)

    def sent(pieces, place, send, recv):
        for step in range(panels - 1):
            for piece in range(pieces):
                for way, block, exists, onward, _ in ways(step):
                    @pl.when(jnp.logical_and(exists, onward))
                    def _(step=step, piece=piece, way=way, block=block):
                        here = place(block, piece)
                        line(way, step, piece, here, here, send, recv).wait_send()

    def accumulate(matrix, block, vectors, kind):
        columns = pl.ds(pl.multiple_of(block * rows, rows), rows)

        @pl.loop(0, rows // tile)
        def _(i):
            part = pl.ds(pl.multiple_of(i * tile, tile), tile)
            product = jnp.dot(matrix[part, columns], vectors[block], preferred_element_type=jnp.float32)
            if kind == "set":
                total[part, :] = product
            elif kind == "add":
                total[part, :] += product
            else:
                total[part, :] -= product

    def rhs_place(block, piece):
        return rhs.at[block, pl.ds(piece * tall, tall)]

    for step in range(panels):
        pass_on(
            step, SOURCE_PIECES, lambda piece: source.at[0, pl.ds(piece * tall, tall)],
            rhs_place, rhs_send, rhs_recv,
        )
        if step == 0:
            load_rhs.wait()
            load_inverse.wait()
            accumulate(inverse_v, panel, rhs, "set")
        else:
            for _, block, exists, _, _ in ways(step):
                @pl.when(exists)
                def _(block=block):
                    accumulate(inverse_v, block, rhs, "add")
    load_coupling.wait()

    def near_place(block, piece):
        return previous.at[block, pl.ds(piece * short, short)]

    def far_arrived(block):
        for piece in range(NEAR, PIECES):
            to_zone(block, piece, near_place(block, piece)).wait_recv()

    @pl.when(has_before)
    def _():
        for step in range(panels):
            if step == 0:
                for piece in range(NEAR):
                    to_zone(panel, piece, near_place(panel, piece)).wait_recv()
                    for way, _, _, onward, _ in ways(0):
                        @pl.when(onward)
                        def _(way=way, piece=piece):
                            here = near_place(panel, piece)
                            line(way, 0, piece, here, here, near_send, near_recv).start()
                far_arrived(panel)
                accumulate(coupling_v, panel, previous, "subtract")
            else:
                pass_on(step, NEAR, None, near_place, near_send, near_recv)
                for _, block, exists, _, _ in ways(step):
                    @pl.when(exists)
                    def _(block=block):
                        far_arrived(block)
                        accumulate(coupling_v, block, previous, "subtract")

    mine[...] = total[...].astype(mine.dtype)
    store = pltpu.make_async_copy(mine, out.at[0], local_sem.at[3])
    store.start()

    def own(piece):
        return mine.at[pl.ds(piece * short, short)]

    def far_place(block, piece):
        return passing.at[block, pl.ds(piece * short, short)]

    def hand_over(block, piece):
        to_zone(block, NEAR + piece, far_place(block, piece)).start()

    @pl.when(has_next)
    def _():
        for piece in range(NEAR):
            to_zone(panel, piece, own(piece)).start()
        for step in range(panels):
            pass_on(
                step, PIECES - NEAR, lambda piece: own(NEAR + piece), far_place, far_send, far_recv, hand_over
            )
            if step == 0:
                for piece in range(NEAR, PIECES):
                    to_zone(panel, piece, own(piece)).start()

    sent(SOURCE_PIECES, rhs_place, rhs_send, rhs_recv)

    @pl.when(has_before)
    def _():
        sent(NEAR, near_place, near_send, near_recv)

    @pl.when(has_next)
    def _():
        sent(PIECES - NEAR, far_place, far_send, far_recv)
        for piece in range(NEAR):
            to_zone(panel, piece, own(piece)).wait_send()
        for block in range(panels):
            for piece in range(NEAR, PIECES):
                to_zone(block, piece, own(piece)).wait_send()
    store.wait()


def solution(mesh):
    panels, zones = mesh.shape["panel"], mesh.shape["zone"]

    def local(source, inverse, coupling):
        _, rows, cols = source.shape
        unknowns = inverse.shape[2]
        far = PIECES - NEAR
        steps = max(panels - 1, 1)
        dma = pltpu.SemaphoreType.DMA
        anywhere = pl.BlockSpec(memory_space=pl.ANY)
        return pl.pallas_call(
            functools.partial(kernel, panels, zones),
            out_shape=jax.ShapeDtypeStruct(source.shape, jnp.bfloat16),
            in_specs=[anywhere] * 3,
            out_specs=anywhere,
            scratch_shapes=[
                pltpu.VMEM((rows, unknowns), jnp.bfloat16),
                pltpu.VMEM((rows, unknowns), jnp.bfloat16),
                pltpu.VMEM((panels, rows, cols), jnp.bfloat16),
                pltpu.VMEM((panels, rows, cols), jnp.bfloat16),
                pltpu.VMEM((panels, rows // PIECES * far, cols), jnp.bfloat16),
                pltpu.VMEM((rows, cols), jnp.float32),
                pltpu.VMEM((rows, cols), jnp.bfloat16),
                dma((4,)),
                dma((2, steps, SOURCE_PIECES)), dma((2, steps, SOURCE_PIECES)),
                dma((2, steps, NEAR)), dma((2, steps, NEAR)),
                dma((2, steps, far)), dma((2, steps, far)),
                dma((panels, PIECES)), dma((panels, PIECES)),
            ],
            compiler_params=pltpu.CompilerParams(
                collective_id=0, has_side_effects=True, vmem_limit_bytes=48 * 2**20
            ),
            cost_estimate=pl.CostEstimate(
                flops=4 * rows * unknowns * cols, bytes_accessed=4 * rows * unknowns, transcendentals=0
            ),
        )(source, inverse, coupling)

    return jax.shard_map(
        local,
        mesh=mesh,
        in_specs=(
            P(("parts", "zone"), "panel", "rhs"),
            P(("parts", "zone"), "panel", None),
            P(("parts", "zone"), "panel", None),
        ),
        out_specs=P(("parts", "zone"), "panel", "rhs"),
        check_vma=False,
    )
```

```python
import functools

import jax
import jax.numpy as jnp
from jax import lax
from jax.experimental import pallas as pl
from jax.experimental.pallas import tpu as pltpu
from jax.sharding import PartitionSpec as P

MESH = pl.DeviceIdType.MESH
RIGHT, LEFT = 0, 1
CHUNKS = 2
SOURCE_PIECES = 4
PIECES = 8
NEAR = (8, 2)
FAR = max(PIECES - near for near in NEAR)


def kernel(
    panels, zones, source, inverse, coupling, out,
    inverse_v, coupling_v, rhs, previous, passing, total, mine,
    local_sem, rhs_send, rhs_recv, near_send, near_recv, far_send, far_recv, zone_send, zone_recv,
):
    panel, zone = lax.axis_index("panel"), lax.axis_index("zone")
    _, rows, width = mine.shape
    tall, short = rows // SOURCE_PIECES, rows // PIECES
    tile = min(rows, 512)
    has_right, has_left = panel < panels - 1, panel > 0
    has_next, has_before = zone < zones - 1, zone > 0

    def columns_of(chunk):
        return pl.ds(chunk * width, width)

    load_rhs = [
        pltpu.make_async_copy(source.at[0, :, columns_of(c)], rhs.at[c, panel], local_sem.at[c])
        for c in range(CHUNKS)
    ]
    load_inverse = pltpu.make_async_copy(inverse.at[0], inverse_v, local_sem.at[CHUNKS])
    load_coupling = pltpu.make_async_copy(coupling.at[0], coupling_v, local_sem.at[CHUNKS + 1])
    for load in load_rhs:
        load.start()

    barrier = pltpu.get_barrier_semaphore()
    count = jnp.int32(0)
    for exists, axis, other in (
        (has_right, "panel", panel + 1),
        (has_left, "panel", panel - 1),
        (has_next, "zone", zone + 1),
        (has_before, "zone", zone - 1),
    ):
        @pl.when(exists)
        def _(axis=axis, other=other):
            pl.semaphore_signal(barrier, inc=1, device_id={axis: other}, device_id_type=MESH)

        count = count + exists.astype(jnp.int32)
    for load in load_rhs:
        load.wait()
    load_inverse.start()
    load_coupling.start()
    pl.semaphore_wait(barrier, count)

    def line(way, chunk, step, piece, here, send, recv, start=None):
        neighbour = panel + 1 if way == RIGHT else panel - 1
        return pltpu.make_async_remote_copy(
            src_ref=here if start is None else start, dst_ref=here,
            send_sem=send.at[chunk, way, step, piece], recv_sem=recv.at[chunk, way, step, piece],
            device_id={"panel": neighbour}, device_id_type=MESH,
        )

    def to_zone(chunk, block, piece, from_ref):
        return pltpu.make_async_remote_copy(
            src_ref=from_ref, dst_ref=previous.at[chunk, block, pl.ds(piece * short, short)],
            send_sem=zone_send.at[chunk, block, piece], recv_sem=zone_recv.at[chunk, block, piece],
            device_id={"zone": zone + 1}, device_id_type=MESH,
        )

    def ways(step):
        return (
            (RIGHT, panel - step, panel - step >= 0, has_right),
            (LEFT, panel + step, panel + step < panels, has_left),
        )

    def pass_on(chunk, step, pieces, place, send, recv, own=None, after=None):
        for piece in range(pieces):
            for way, block, exists, onward in ways(step):
                @pl.when(exists)
                def _(piece=piece, way=way, block=block, onward=onward):
                    here = place(chunk, block, piece)
                    if step > 0:
                        line(way, chunk, step - 1, piece, here, send, recv).wait_recv()
                    if step < panels - 1:
                        @pl.when(onward)
                        def _():
                            start = own(piece) if own is not None else None
                            line(way, chunk, step, piece, here, send, recv, start).start()
                    if step > 0 and after is not None:
                        after(block, piece)
            if step == 0 and after is not None:
                after(panel, piece)

    def sent(chunk, pieces, place, send, recv):
        for step in range(panels - 1):
            for piece in range(pieces):
                for way, block, exists, onward in ways(step):
                    @pl.when(jnp.logical_and(exists, onward))
                    def _(step=step, piece=piece, way=way, block=block):
                        line(way, chunk, step, piece, place(chunk, block, piece), send, recv).wait_send()

    def accumulate(matrix, chunk, block, vectors, kind):
        columns = pl.ds(pl.multiple_of(block * rows, rows), rows)

        @pl.loop(0, rows // tile)
        def _(i):
            part = pl.ds(pl.multiple_of(i * tile, tile), tile)
            product = jnp.dot(matrix[part, columns], vectors[chunk, block], preferred_element_type=jnp.float32)
            if kind == "set":
                total[chunk, part, :] = product
            elif kind == "add":
                total[chunk, part, :] += product
            else:
                total[chunk, part, :] -= product

    def rhs_place(chunk, block, piece):
        return rhs.at[chunk, block, pl.ds(piece * tall, tall)]

    def rhs_pass(chunk, step):
        pass_on(chunk, step, SOURCE_PIECES, rhs_place, rhs_send, rhs_recv)

    def rhs_product(chunk, step):
        if step == 0:
            accumulate(inverse_v, chunk, panel, rhs, "set")
        else:
            for _, block, exists, _ in ways(step):
                @pl.when(exists)
                def _(block=block):
                    accumulate(inverse_v, chunk, block, rhs, "add")

    def near_place(chunk, block, piece):
        return previous.at[chunk, block, pl.ds(piece * short, short)]

    def previous_pass(chunk, step):
        if step == 0:
            for piece in range(NEAR[chunk]):
                here = near_place(chunk, panel, piece)
                to_zone(chunk, panel, piece, here).wait_recv()
                if panels > 1:
                    for way, _, _, onward in ways(0):
                        @pl.when(onward)
                        def _(way=way, piece=piece, here=here):
                            line(way, chunk, 0, piece, here, near_send, near_recv).start()
        else:
            pass_on(chunk, step, NEAR[chunk], near_place, near_send, near_recv)

    def previous_product(chunk, step):
        def one(block):
            for piece in range(NEAR[chunk], PIECES):
                to_zone(chunk, block, piece, near_place(chunk, block, piece)).wait_recv()
            accumulate(coupling_v, chunk, block, previous, "subtract")

        if step == 0:
            one(panel)
        else:
            for _, block, exists, _ in ways(step):
                @pl.when(exists)
                def _(block=block):
                    one(block)

    def own(chunk, piece):
        return mine.at[chunk, pl.ds(piece * short, short)]

    def far_place(chunk, block, piece):
        return passing.at[block, pl.ds(piece * short, short)]

    def finish(chunk):
        result = total[chunk].astype(mine.dtype)
        out[0, :, columns_of(chunk)] = result

        @pl.when(has_next)
        def _():
            mine[chunk] = result
            near = NEAR[chunk]
            for piece in range(near):
                to_zone(chunk, panel, piece, own(chunk, piece)).start()

            def hand_over(block, piece):
                from_ref = own(chunk, near + piece) if step == 0 else far_place(chunk, block, piece)
                to_zone(chunk, block, near + piece, from_ref).start()

            if near < PIECES:
                for step in range(panels):
                    pass_on(
                        chunk, step, PIECES - near, far_place, far_send, far_recv,
                        (lambda piece: own(chunk, near + piece)) if step == 0 else None, hand_over,
                    )

    rhs_pass(0, 0)
    load_inverse.wait()
    rhs_product(0, 0)
    for step in range(1, panels):
        if step == panels - 1:
            rhs_pass(1, 0)
        rhs_pass(0, step)
        rhs_product(0, step)
    if panels == 1:
        rhs_pass(1, 0)

    @pl.when(jnp.logical_not(has_before))
    def _():
        finish(0)

    load_coupling.wait()
    for step in range(panels):
        if step > 0:
            rhs_pass(1, step)

        @pl.when(has_before)
        def _(step=step):
            previous_pass(0, step)

        rhs_product(1, step)

        @pl.when(has_before)
        def _(step=step):
            previous_product(0, step)

    @pl.when(has_before)
    def _():
        finish(0)
        for step in range(panels):
            previous_pass(1, step)
            previous_product(1, step)

    finish(1)

    for chunk in range(CHUNKS):
        sent(chunk, SOURCE_PIECES, rhs_place, rhs_send, rhs_recv)

        @pl.when(has_before)
        def _(chunk=chunk):
            sent(chunk, NEAR[chunk], near_place, near_send, near_recv)

        @pl.when(has_next)
        def _(chunk=chunk):
            sent(chunk, PIECES - NEAR[chunk], far_place, far_send, far_recv)
            for piece in range(NEAR[chunk]):
                to_zone(chunk, panel, piece, own(chunk, piece)).wait_send()
            for block in range(panels):
                for piece in range(NEAR[chunk], PIECES):
                    to_zone(chunk, block, piece, own(chunk, piece)).wait_send()


def solution(mesh):
    panels, zones = mesh.shape["panel"], mesh.shape["zone"]

    def local(source, inverse, coupling):
        _, rows, cols = source.shape
        unknowns = inverse.shape[2]
        width = cols // CHUNKS
        steps = max(panels - 1, 1)
        dma = pltpu.SemaphoreType.DMA
        anywhere = pl.BlockSpec(memory_space=pltpu.HBM)
        return pl.pallas_call(
            functools.partial(kernel, panels, zones),
            out_shape=jax.ShapeDtypeStruct(source.shape, jnp.bfloat16),
            in_specs=[anywhere] * 3,
            out_specs=pl.BlockSpec(memory_space=pltpu.VMEM),
            scratch_shapes=[
                pltpu.VMEM((rows, unknowns), jnp.bfloat16),
                pltpu.VMEM((rows, unknowns), jnp.bfloat16),
                pltpu.VMEM((CHUNKS, panels, rows, width), jnp.bfloat16),
                pltpu.VMEM((CHUNKS, panels, rows, width), jnp.bfloat16),
                pltpu.VMEM((panels, rows // PIECES * FAR, width), jnp.bfloat16),
                pltpu.VMEM((CHUNKS, rows, width), jnp.float32),
                pltpu.VMEM((CHUNKS, rows, width), jnp.bfloat16),
                dma((CHUNKS + 2,)),
                dma((CHUNKS, 2, steps, SOURCE_PIECES)), dma((CHUNKS, 2, steps, SOURCE_PIECES)),
                dma((CHUNKS, 2, steps, PIECES)), dma((CHUNKS, 2, steps, PIECES)),
                dma((CHUNKS, 2, steps, FAR)), dma((CHUNKS, 2, steps, FAR)),
                dma((CHUNKS, panels, PIECES)), dma((CHUNKS, panels, PIECES)),
            ],
            compiler_params=pltpu.CompilerParams(
                collective_id=0, has_side_effects=True, vmem_limit_bytes=64 * 2**20 - 2**18
            ),
            cost_estimate=pl.CostEstimate(
                flops=4 * rows * unknowns * cols, bytes_accessed=4 * rows * unknowns, transcendentals=0
            ),
        )(source, inverse, coupling)

    return jax.shard_map(
        local,
        mesh=mesh,
        in_specs=(
            P(("parts", "zone"), "panel", "rhs"),
            P(("parts", "zone"), "panel", None),
            P(("parts", "zone"), "panel", None),
        ),
        out_specs=P(("parts", "zone"), "panel", "rhs"),
        check_vma=False,
    )
```

```python
import functools

import jax
import jax.numpy as jnp
from jax import lax
from jax.experimental import pallas as pl
from jax.experimental.pallas import tpu as pltpu
from jax.sharding import PartitionSpec as P

MESH = pl.DeviceIdType.MESH
RIGHT, LEFT = 0, 1
CHUNKS = 2
SOURCE_PIECES = 4
PIECES = 8
NEAR = (8, 2)
FAR = max(PIECES - near for near in NEAR)


def kernel(
    panels, zones, source, inverse, coupling, out,
    inverse_v, coupling_v, rhs, previous, passing, total, mine,
    local_sem, rhs_send, rhs_recv, near_send, near_recv, far_send, far_recv, zone_send, zone_recv,
):
    panel, zone = lax.axis_index("panel"), lax.axis_index("zone")
    _, rows, width = mine.shape
    tall, short = rows // SOURCE_PIECES, rows // PIECES
    tile = min(rows, 512)
    has_right, has_left = panel < panels - 1, panel > 0
    has_next, has_before = zone < zones - 1, zone > 0

    def columns_of(chunk):
        return pl.ds(chunk * width, width)

    load_rhs = [
        pltpu.make_async_copy(source.at[0, :, columns_of(c)], rhs.at[c, panel], local_sem.at[c])
        for c in range(CHUNKS)
    ]
    load_inverse = pltpu.make_async_copy(inverse.at[0], inverse_v, local_sem.at[CHUNKS])
    load_coupling = pltpu.make_async_copy(coupling.at[0], coupling_v, local_sem.at[CHUNKS + 1])
    for load in load_rhs:
        load.start()

    barrier = pltpu.get_barrier_semaphore()
    count = jnp.int32(0)
    for exists, axis, other in (
        (has_right, "panel", panel + 1),
        (has_left, "panel", panel - 1),
        (has_next, "zone", zone + 1),
        (has_before, "zone", zone - 1),
    ):
        @pl.when(exists)
        def _(axis=axis, other=other):
            pl.semaphore_signal(barrier, inc=1, device_id={axis: other}, device_id_type=MESH)

        count = count + exists.astype(jnp.int32)
    for load in load_rhs:
        load.wait()
    load_inverse.start()
    load_coupling.start()
    pl.semaphore_wait(barrier, count)

    def line(way, chunk, step, piece, here, send, recv, start=None):
        neighbour = panel + 1 if way == RIGHT else panel - 1
        return pltpu.make_async_remote_copy(
            src_ref=here if start is None else start, dst_ref=here,
            send_sem=send.at[chunk, way, step, piece], recv_sem=recv.at[chunk, way, step, piece],
            device_id={"panel": neighbour}, device_id_type=MESH,
        )

    def to_zone(chunk, block, piece, from_ref):
        return pltpu.make_async_remote_copy(
            src_ref=from_ref, dst_ref=previous.at[chunk, block, pl.ds(piece * short, short)],
            send_sem=zone_send.at[chunk, block, piece], recv_sem=zone_recv.at[chunk, block, piece],
            device_id={"zone": zone + 1}, device_id_type=MESH,
        )

    def ways(step):
        return (
            (RIGHT, panel - step, panel - step >= 0, has_right),
            (LEFT, panel + step, panel + step < panels, has_left),
        )

    def pass_on(chunk, step, pieces, place, send, recv, own=None, after=None):
        for piece in range(pieces):
            for way, block, exists, onward in ways(step):
                @pl.when(exists)
                def _(piece=piece, way=way, block=block, onward=onward):
                    here = place(chunk, block, piece)
                    if step > 0:
                        line(way, chunk, step - 1, piece, here, send, recv).wait_recv()
                    if step < panels - 1:
                        @pl.when(onward)
                        def _():
                            start = own(piece) if own is not None else None
                            line(way, chunk, step, piece, here, send, recv, start).start()
                    if step > 0 and after is not None:
                        after(block, piece)
            if step == 0 and after is not None:
                after(panel, piece)

    def sent(chunk, pieces, place, send, recv):
        for step in range(panels - 1):
            for piece in range(pieces):
                for way, block, exists, onward in ways(step):
                    @pl.when(jnp.logical_and(exists, onward))
                    def _(step=step, piece=piece, way=way, block=block):
                        line(way, chunk, step, piece, place(chunk, block, piece), send, recv).wait_send()

    def accumulate(matrix, chunks, block, vectors, kind):
        columns = pl.ds(pl.multiple_of(block * rows, rows), rows)

        @pl.loop(0, rows // tile)
        def _(i):
            part = pl.ds(pl.multiple_of(i * tile, tile), tile)
            wide = jnp.concatenate([vectors[c, block] for c in chunks], axis=1)
            product = jnp.dot(matrix[part, columns], wide, preferred_element_type=jnp.float32)
            for n, c in enumerate(chunks):
                one = product[:, n * width:(n + 1) * width]
                if kind == "set":
                    total[c, part, :] = one
                elif kind == "add":
                    total[c, part, :] += one
                else:
                    total[c, part, :] -= one

    def rhs_place(chunk, block, piece):
        return rhs.at[chunk, block, pl.ds(piece * tall, tall)]

    def rhs_pass(chunk, step):
        pass_on(chunk, step, SOURCE_PIECES, rhs_place, rhs_send, rhs_recv)

    def rhs_product(chunks, step):
        if step == 0:
            accumulate(inverse_v, chunks, panel, rhs, "set")
        else:
            for _, block, exists, _ in ways(step):
                @pl.when(exists)
                def _(block=block):
                    accumulate(inverse_v, chunks, block, rhs, "add")

    def near_place(chunk, block, piece):
        return previous.at[chunk, block, pl.ds(piece * short, short)]

    def previous_pass(chunk, step):
        if step == 0:
            for piece in range(NEAR[chunk]):
                here = near_place(chunk, panel, piece)
                to_zone(chunk, panel, piece, here).wait_recv()
                if panels > 1:
                    for way, _, _, onward in ways(0):
                        @pl.when(onward)
                        def _(way=way, piece=piece, here=here):
                            line(way, chunk, 0, piece, here, near_send, near_recv).start()
        else:
            pass_on(chunk, step, NEAR[chunk], near_place, near_send, near_recv)

    def previous_product(step):
        def one(block):
            for chunk in range(CHUNKS):
                for piece in range(NEAR[chunk], PIECES):
                    to_zone(chunk, block, piece, near_place(chunk, block, piece)).wait_recv()
            accumulate(coupling_v, (0, 1), block, previous, "subtract")

        if step == 0:
            one(panel)
        else:
            for _, block, exists, _ in ways(step):
                @pl.when(exists)
                def _(block=block):
                    one(block)

    def own(chunk, piece):
        return mine.at[chunk, pl.ds(piece * short, short)]

    def far_place(chunk, block, piece):
        return passing.at[block, pl.ds(piece * short, short)]

    def finish(chunk):
        result = total[chunk].astype(mine.dtype)
        out[0, :, columns_of(chunk)] = result

        @pl.when(has_next)
        def _():
            mine[chunk] = result
            near = NEAR[chunk]
            for piece in range(near):
                to_zone(chunk, panel, piece, own(chunk, piece)).start()

            def hand_over(block, piece):
                from_ref = own(chunk, near + piece) if step == 0 else far_place(chunk, block, piece)
                to_zone(chunk, block, near + piece, from_ref).start()

            if near < PIECES:
                for step in range(panels):
                    pass_on(
                        chunk, step, PIECES - near, far_place, far_send, far_recv,
                        (lambda piece: own(chunk, near + piece)) if step == 0 else None, hand_over,
                    )

    last = panels - 1
    is_first = jnp.logical_not(has_before)

    def in_first(action):
        pl.when(is_first)(action)

    def in_later(action):
        pl.when(has_before)(action)

    rhs_pass(0, 0)
    for step in range(1, panels):
        rhs_pass(0, step)
        if step == 1:
            rhs_pass(1, 0)
            load_inverse.wait()
        if step == last:
            @in_first
            def _(step=step):
                rhs_product((0,), step - 1)
                rhs_product((0,), step)
                finish(0)
        if step > 1:
            rhs_pass(1, step - 1)

        @in_first
        def _(step=step):
            if step < last:
                rhs_product((0,), step - 1)
            rhs_product((1,), step - 1)

        if step == last:
            @in_later
            def _():
                previous_pass(0, 0)

        @in_later
        def _(step=step):
            rhs_product((0, 1), step - 1)

    if panels == 1:
        rhs_pass(1, 0)
        load_inverse.wait()

        @in_first
        def _():
            rhs_product((0,), 0)
            finish(0)

        @in_later
        def _():
            previous_pass(0, 0)
    else:
        rhs_pass(1, last)

    @in_first
    def _():
        rhs_product((1,), last)
        load_coupling.wait()

    @in_later
    def _():
        if last >= 1:
            previous_pass(0, 1)
        rhs_product((0, 1), last)
        load_coupling.wait()
        previous_pass(1, 0)
        for step in range(2, panels):
            previous_pass(0, step)
            previous_pass(1, step - 1)
            if step == 2:
                previous_product(0)
            previous_product(step - 1)
        if last <= 1:
            previous_product(0)
        if last >= 1:
            previous_pass(1, last)
            previous_product(last)
        finish(0)

    finish(1)

    for chunk in range(CHUNKS):
        sent(chunk, SOURCE_PIECES, rhs_place, rhs_send, rhs_recv)

        @pl.when(has_before)
        def _(chunk=chunk):
            sent(chunk, NEAR[chunk], near_place, near_send, near_recv)

        @pl.when(has_next)
        def _(chunk=chunk):
            sent(chunk, PIECES - NEAR[chunk], far_place, far_send, far_recv)
            for piece in range(NEAR[chunk]):
                to_zone(chunk, panel, piece, own(chunk, piece)).wait_send()
            for block in range(panels):
                for piece in range(NEAR[chunk], PIECES):
                    to_zone(chunk, block, piece, own(chunk, piece)).wait_send()


def solution(mesh):
    panels, zones = mesh.shape["panel"], mesh.shape["zone"]

    def local(source, inverse, coupling):
        _, rows, cols = source.shape
        unknowns = inverse.shape[2]
        width = cols // CHUNKS
        steps = max(panels - 1, 1)
        dma = pltpu.SemaphoreType.DMA
        anywhere = pl.BlockSpec(memory_space=pltpu.HBM)
        return pl.pallas_call(
            functools.partial(kernel, panels, zones),
            out_shape=jax.ShapeDtypeStruct(source.shape, jnp.bfloat16),
            in_specs=[anywhere] * 3,
            out_specs=pl.BlockSpec(memory_space=pltpu.VMEM),
            scratch_shapes=[
                pltpu.VMEM((rows, unknowns), jnp.bfloat16),
                pltpu.VMEM((rows, unknowns), jnp.bfloat16),
                pltpu.VMEM((CHUNKS, panels, rows, width), jnp.bfloat16),
                pltpu.VMEM((CHUNKS, panels, rows, width), jnp.bfloat16),
                pltpu.VMEM((panels, rows // PIECES * FAR, width), jnp.bfloat16),
                pltpu.VMEM((CHUNKS, rows, width), jnp.float32),
                pltpu.VMEM((CHUNKS, rows, width), jnp.bfloat16),
                dma((CHUNKS + 2,)),
                dma((CHUNKS, 2, steps, SOURCE_PIECES)), dma((CHUNKS, 2, steps, SOURCE_PIECES)),
                dma((CHUNKS, 2, steps, PIECES)), dma((CHUNKS, 2, steps, PIECES)),
                dma((CHUNKS, 2, steps, FAR)), dma((CHUNKS, 2, steps, FAR)),
                dma((CHUNKS, panels, PIECES)), dma((CHUNKS, panels, PIECES)),
            ],
            compiler_params=pltpu.CompilerParams(
                collective_id=0, has_side_effects=True, vmem_limit_bytes=48 * 2**20
            ),
            cost_estimate=pl.CostEstimate(
                flops=4 * rows * unknowns * cols, bytes_accessed=4 * rows * unknowns, transcendentals=0
            ),
        )(source, inverse, coupling)

    return jax.shard_map(
        local,
        mesh=mesh,
        in_specs=(
            P(("parts", "zone"), "panel", "rhs"),
            P(("parts", "zone"), "panel", None),
            P(("parts", "zone"), "panel", None),
        ),
        out_specs=P(("parts", "zone"), "panel", "rhs"),
        check_vma=False,
    )
```

```python
import functools

import jax
import jax.numpy as jnp
from jax import lax
from jax.experimental import pallas as pl
from jax.experimental.pallas import tpu as pltpu
from jax.sharding import PartitionSpec as P

MESH = pl.DeviceIdType.MESH
RIGHT, LEFT = 0, 1
CHUNKS = 2
SOURCE_PIECES = 4
PIECES = 8
NEAR = (8, 2)
FAR = max(PIECES - near for near in NEAR)


def kernel(
    panels, zones, source, inverse, coupling, out,
    inverse_v, coupling_v, rhs, previous, passing, total, mine,
    local_sem, rhs_send, rhs_recv, near_send, near_recv, far_send, far_recv, zone_send, zone_recv,
):
    panel, zone = lax.axis_index("panel"), lax.axis_index("zone")
    _, rows, width = mine.shape
    tall, short = rows // SOURCE_PIECES, rows // PIECES
    tile = min(rows, 512)
    has_right, has_left = panel < panels - 1, panel > 0
    has_next, has_before = zone < zones - 1, zone > 0

    def columns_of(chunk):
        return pl.ds(chunk * width, width)

    load_rhs = [
        pltpu.make_async_copy(source.at[0, :, columns_of(c)], rhs.at[c, panel], local_sem.at[c])
        for c in range(CHUNKS)
    ]
    load_inverse = pltpu.make_async_copy(inverse.at[0], inverse_v, local_sem.at[CHUNKS])
    load_coupling = pltpu.make_async_copy(coupling.at[0], coupling_v, local_sem.at[CHUNKS + 1])
    for load in load_rhs:
        load.start()

    barrier = pltpu.get_barrier_semaphore()
    count = jnp.int32(0)
    for exists, axis, other in (
        (has_right, "panel", panel + 1),
        (has_left, "panel", panel - 1),
        (has_next, "zone", zone + 1),
        (has_before, "zone", zone - 1),
    ):
        @pl.when(exists)
        def _(axis=axis, other=other):
            pl.semaphore_signal(barrier, inc=1, device_id={axis: other}, device_id_type=MESH)

        count = count + exists.astype(jnp.int32)
    for load in load_rhs:
        load.wait()
    load_inverse.start()
    load_coupling.start()
    pl.semaphore_wait(barrier, count)

    def line(way, chunk, step, piece, here, send, recv, start=None):
        neighbour = panel + 1 if way == RIGHT else panel - 1
        return pltpu.make_async_remote_copy(
            src_ref=here if start is None else start, dst_ref=here,
            send_sem=send.at[chunk, way, step, piece], recv_sem=recv.at[chunk, way, step, piece],
            device_id={"panel": neighbour}, device_id_type=MESH,
        )

    def to_zone(chunk, block, piece, from_ref):
        return pltpu.make_async_remote_copy(
            src_ref=from_ref, dst_ref=previous.at[chunk, block, pl.ds(piece * short, short)],
            send_sem=zone_send.at[chunk, block, piece], recv_sem=zone_recv.at[chunk, block, piece],
            device_id={"zone": zone + 1}, device_id_type=MESH,
        )

    def ways(step):
        return (
            (RIGHT, panel - step, panel - step >= 0, has_right),
            (LEFT, panel + step, panel + step < panels, has_left),
        )

    def pass_on(chunk, step, pieces, place, send, recv, own=None, after=None):
        for piece in pieces:
            for way, block, exists, onward in ways(step):
                @pl.when(exists)
                def _(piece=piece, way=way, block=block, onward=onward):
                    here = place(chunk, block, piece)
                    if step > 0:
                        line(way, chunk, step - 1, piece, here, send, recv).wait_recv()
                    if step < panels - 1:
                        @pl.when(onward)
                        def _():
                            start = own(piece) if own is not None else None
                            line(way, chunk, step, piece, here, send, recv, start).start()
                    if step > 0 and after is not None:
                        after(block, piece)

    def sent(chunk, pieces, place, send, recv):
        for step in range(panels - 1):
            for piece in range(pieces):
                for way, block, exists, onward in ways(step):
                    @pl.when(jnp.logical_and(exists, onward))
                    def _(step=step, piece=piece, way=way, block=block):
                        line(way, chunk, step, piece, place(chunk, block, piece), send, recv).wait_send()

    def accumulate(matrix, chunks, block, vectors, kind, part_of=0, parts=1):
        depth = rows // parts
        columns = pl.ds(pl.multiple_of(block * rows + part_of * depth, depth), depth)
        inside = pl.ds(part_of * depth, depth)

        @pl.loop(0, rows // tile)
        def _(i):
            part = pl.ds(pl.multiple_of(i * tile, tile), tile)
            wide = jnp.concatenate([vectors[c, block, inside] for c in chunks], axis=1)
            product = jnp.dot(matrix[part, columns], wide, preferred_element_type=jnp.float32)
            for n, c in enumerate(chunks):
                one = product[:, n * width:(n + 1) * width]
                if kind == "set":
                    total[c, part, :] = one
                elif kind == "add":
                    total[c, part, :] += one
                else:
                    total[c, part, :] -= one

    def rhs_place(chunk, block, piece):
        return rhs.at[chunk, block, pl.ds(piece * tall, tall)]

    def rhs_pass(chunk, step, pieces=range(SOURCE_PIECES)):
        pass_on(chunk, step, pieces, rhs_place, rhs_send, rhs_recv)

    def rhs_product(chunks, step, *quarter):
        if step == 0:
            accumulate(inverse_v, chunks, panel, rhs, "set", *quarter)
        else:
            for _, block, exists, _ in ways(step):
                @pl.when(exists)
                def _(block=block):
                    accumulate(inverse_v, chunks, block, rhs, "add", *quarter)

    def near_place(chunk, block, piece):
        return previous.at[chunk, block, pl.ds(piece * short, short)]

    def previous_pass(chunk, step):
        if step == 0:
            for piece in range(NEAR[chunk]):
                here = near_place(chunk, panel, piece)
                to_zone(chunk, panel, piece, here).wait_recv()
                if panels > 1:
                    for way, _, _, onward in ways(0):
                        @pl.when(onward)
                        def _(way=way, piece=piece, here=here):
                            line(way, chunk, 0, piece, here, near_send, near_recv).start()
        else:
            pass_on(chunk, step, range(NEAR[chunk]), near_place, near_send, near_recv)

    def previous_product(step):
        parts = quarters if step == last and step > 0 else 1

        def one(block):
            for part in range(parts):
                for chunk in range(CHUNKS):
                    for piece in range(part * PIECES // parts, (part + 1) * PIECES // parts):
                        if piece >= NEAR[chunk]:
                            to_zone(chunk, block, piece, near_place(chunk, block, piece)).wait_recv()
                accumulate(coupling_v, (0, 1), block, previous, "subtract", part, parts)

        if step == 0:
            one(panel)
        else:
            for _, block, exists, _ in ways(step):
                @pl.when(exists)
                def _(block=block):
                    one(block)

    def own(chunk, piece):
        return mine.at[chunk, pl.ds(piece * short, short)]

    def far_place(chunk, block, piece):
        return passing.at[block, pl.ds(piece * short, short)]

    def source_sent():
        for chunk in range(CHUNKS):
            sent(chunk, SOURCE_PIECES, rhs_place, rhs_send, rhs_recv)

    def finish(chunk):
        @pl.when(has_next)
        def _():
            mine[chunk] = total[chunk].astype(mine.dtype)
            near = NEAR[chunk]
            for piece in range(PIECES):
                to_zone(chunk, panel, piece, own(chunk, piece)).start()

            def hand_over(block, piece):
                to_zone(chunk, block, near + piece, far_place(chunk, block, piece)).start()

            if chunk == CHUNKS - 1:
                source_sent()
            if near < PIECES:
                for step in range(panels):
                    pass_on(
                        chunk, step, range(PIECES - near), far_place, far_send, far_recv,
                        (lambda piece: own(chunk, near + piece)) if step == 0 else None, hand_over,
                    )

        out[0, :, columns_of(chunk)] = total[chunk].astype(out.dtype)

    last, quarters = panels - 1, min(4, rows // 128)
    is_first = jnp.logical_not(has_before)

    def in_first(action):
        pl.when(is_first)(action)

    def in_later(action):
        pl.when(has_before)(action)

    rhs_pass(0, 0)
    for step in range(1, panels):
        rhs_pass(0, step)
        if step == 1:
            rhs_pass(1, 0)
            load_inverse.wait()
        if step == last:
            @in_first
            def _(step=step):
                rhs_product((0,), step - 1)
                rhs_product((0,), step)
                finish(0)
        if step > 1:
            rhs_pass(1, step - 1)

        @in_first
        def _(step=step):
            if step < last:
                rhs_product((0,), step - 1)
            rhs_product((1,), step - 1)

        if step == last:
            @in_later
            def _():
                previous_pass(0, 0)

        @in_later
        def _(step=step):
            rhs_product((0, 1), step - 1)

    if panels == 1:
        rhs_pass(1, 0)
        load_inverse.wait()

        @in_first
        def _():
            rhs_product((0,), 0)
            finish(0)

        @in_later
        def _():
            previous_pass(0, 0)
        @in_first
        def _():
            rhs_product((1,), 0)
    else:
        each = SOURCE_PIECES // quarters
        for part in range(quarters):
            rhs_pass(1, last, range(part * each, (part + 1) * each))

            @in_first
            def _(part=part):
                rhs_product((1,), last, part, quarters)

    @in_first
    def _():
        load_coupling.wait()

    @in_later
    def _():
        if last >= 1:
            previous_pass(0, 1)
        rhs_product((0, 1), last)
        load_coupling.wait()
        previous_pass(1, 0)
        for step in range(2, panels):
            previous_pass(0, step)
            previous_pass(1, step - 1)
            if step == 2:
                previous_product(0)
            previous_product(step - 1)
        if last <= 1:
            previous_product(0)
        if last >= 1:
            previous_pass(1, last)
            previous_product(last)
        finish(0)

    finish(1)

    pl.when(jnp.logical_not(has_next))(source_sent)
    for chunk in range(CHUNKS):
        @pl.when(has_before)
        def _(chunk=chunk):
            sent(chunk, NEAR[chunk], near_place, near_send, near_recv)

        @pl.when(has_next)
        def _(chunk=chunk):
            sent(chunk, PIECES - NEAR[chunk], far_place, far_send, far_recv)
            for piece in range(NEAR[chunk]):
                to_zone(chunk, panel, piece, own(chunk, piece)).wait_send()
            for block in range(panels):
                for piece in range(NEAR[chunk], PIECES):
                    to_zone(chunk, block, piece, own(chunk, piece)).wait_send()


def solution(mesh):
    panels, zones = mesh.shape["panel"], mesh.shape["zone"]

    def local(source, inverse, coupling):
        _, rows, cols = source.shape
        unknowns = inverse.shape[2]
        width = cols // CHUNKS
        steps = max(panels - 1, 1)
        dma = pltpu.SemaphoreType.DMA
        anywhere = pl.BlockSpec(memory_space=pltpu.HBM)
        return pl.pallas_call(
            functools.partial(kernel, panels, zones),
            out_shape=jax.ShapeDtypeStruct(source.shape, jnp.bfloat16),
            in_specs=[anywhere] * 3,
            out_specs=pl.BlockSpec(memory_space=pltpu.VMEM),
            scratch_shapes=[
                pltpu.VMEM((rows, unknowns), jnp.bfloat16),
                pltpu.VMEM((rows, unknowns), jnp.bfloat16),
                pltpu.VMEM((CHUNKS, panels, rows, width), jnp.bfloat16),
                pltpu.VMEM((CHUNKS, panels, rows, width), jnp.bfloat16),
                pltpu.VMEM((panels, rows // PIECES * FAR, width), jnp.bfloat16),
                pltpu.VMEM((CHUNKS, rows, width), jnp.float32),
                pltpu.VMEM((CHUNKS, rows, width), jnp.bfloat16),
                dma((CHUNKS + 2,)),
                dma((CHUNKS, 2, steps, SOURCE_PIECES)), dma((CHUNKS, 2, steps, SOURCE_PIECES)),
                dma((CHUNKS, 2, steps, PIECES)), dma((CHUNKS, 2, steps, PIECES)),
                dma((CHUNKS, 2, steps, FAR)), dma((CHUNKS, 2, steps, FAR)),
                dma((CHUNKS, panels, PIECES)), dma((CHUNKS, panels, PIECES)),
            ],
            compiler_params=pltpu.CompilerParams(
                collective_id=0, has_side_effects=True, vmem_limit_bytes=48 * 2**20
            ),
            cost_estimate=pl.CostEstimate(
                flops=4 * rows * unknowns * cols, bytes_accessed=4 * rows * unknowns, transcendentals=0
            ),
        )(source, inverse, coupling)

    return jax.shard_map(
        local,
        mesh=mesh,
        in_specs=(
            P(("parts", "zone"), "panel", "rhs"),
            P(("parts", "zone"), "panel", None),
            P(("parts", "zone"), "panel", None),
        ),
        out_specs=P(("parts", "zone"), "panel", "rhs"),
        check_vma=False,
    )
```

```python
import functools

import jax
import jax.numpy as jnp
from jax import lax
from jax.experimental import pallas as pl
from jax.experimental.pallas import tpu as pltpu
from jax.sharding import PartitionSpec as P

MESH = pl.DeviceIdType.MESH
RIGHT, LEFT = 0, 1
CHUNKS = 2
SOURCE_PIECES = 4
PIECES = 8
NEAR = (8, 2)
FAR = max(PIECES - near for near in NEAR)


def kernel(
    panels, zones, source, inverse, coupling, out,
    inverse_v, coupling_v, rhs, previous, passing, total, mine,
    local_sem, rhs_send, rhs_recv, near_send, near_recv, far_send, far_recv, zone_send, zone_recv,
):
    panel, zone = lax.axis_index("panel"), lax.axis_index("zone")
    _, rows, width = mine.shape
    tall, short = rows // SOURCE_PIECES, rows // PIECES
    tile = min(rows, 512)
    has_right, has_left = panel < panels - 1, panel > 0
    has_next, has_before = zone < zones - 1, zone > 0

    def columns_of(chunk):
        return pl.ds(chunk * width, width)

    load_rhs = [
        pltpu.make_async_copy(source.at[0, :, columns_of(c)], rhs.at[c, panel], local_sem.at[c])
        for c in range(CHUNKS)
    ]
    load_inverse = pltpu.make_async_copy(inverse.at[0], inverse_v, local_sem.at[CHUNKS])
    load_coupling = pltpu.make_async_copy(coupling.at[0], coupling_v, local_sem.at[CHUNKS + 1])
    for load in load_rhs:
        load.start()

    barrier = pltpu.get_barrier_semaphore()
    count = jnp.int32(0)
    for exists, axis, other in (
        (has_right, "panel", panel + 1),
        (has_left, "panel", panel - 1),
        (has_next, "zone", zone + 1),
        (has_before, "zone", zone - 1),
    ):
        @pl.when(exists)
        def _(axis=axis, other=other):
            pl.semaphore_signal(barrier, inc=1, device_id={axis: other}, device_id_type=MESH)

        count = count + exists.astype(jnp.int32)
    for load in load_rhs:
        load.wait()
    load_inverse.start()
    load_coupling.start()
    pl.semaphore_wait(barrier, count)

    def line(way, chunk, step, piece, here, send, recv, start=None):
        neighbour = panel + 1 if way == RIGHT else panel - 1
        return pltpu.make_async_remote_copy(
            src_ref=here if start is None else start, dst_ref=here,
            send_sem=send.at[chunk, way, step, piece], recv_sem=recv.at[chunk, way, step, piece],
            device_id={"panel": neighbour}, device_id_type=MESH,
        )

    def to_zone(chunk, block, piece, from_ref):
        return pltpu.make_async_remote_copy(
            src_ref=from_ref, dst_ref=previous.at[chunk, block, pl.ds(piece * short, short)],
            send_sem=zone_send.at[chunk, block, piece], recv_sem=zone_recv.at[chunk, block, piece],
            device_id={"zone": zone + 1}, device_id_type=MESH,
        )

    def ways(step):
        return (
            (RIGHT, panel - step, panel - step >= 0, has_right),
            (LEFT, panel + step, panel + step < panels, has_left),
        )

    def pass_on(chunk, step, pieces, place, send, recv, own=None, after=None):
        for piece in pieces:
            for way, block, exists, onward in ways(step):
                @pl.when(exists)
                def _(piece=piece, way=way, block=block, onward=onward):
                    here = place(chunk, block, piece)
                    if step > 0:
                        line(way, chunk, step - 1, piece, here, send, recv).wait_recv()
                    if step < panels - 1:
                        @pl.when(onward)
                        def _():
                            start = own(piece) if own is not None else None
                            line(way, chunk, step, piece, here, send, recv, start).start()
                    if step > 0 and after is not None:
                        after(block, piece)
            if step == 0 and after is not None:
                after(panel, piece)

    def sent(chunk, pieces, place, send, recv):
        for step in range(panels - 1):
            for piece in range(pieces):
                for way, block, exists, onward in ways(step):
                    @pl.when(jnp.logical_and(exists, onward))
                    def _(step=step, piece=piece, way=way, block=block):
                        line(way, chunk, step, piece, place(chunk, block, piece), send, recv).wait_send()

    def accumulate(matrix, chunks, block, vectors, kind, part_of=0, parts=1):
        depth = rows // parts
        columns = pl.ds(pl.multiple_of(block * rows + part_of * depth, depth), depth)
        inside = pl.ds(part_of * depth, depth)

        @pl.loop(0, rows // tile)
        def _(i):
            part = pl.ds(pl.multiple_of(i * tile, tile), tile)
            wide = jnp.concatenate([vectors[c, block, inside] for c in chunks], axis=1)
            product = jnp.dot(matrix[part, columns], wide, preferred_element_type=jnp.float32)
            for n, c in enumerate(chunks):
                one = product[:, n * width:(n + 1) * width]
                if kind == "set":
                    total[c, part, :] = one
                elif kind == "add":
                    total[c, part, :] += one
                else:
                    total[c, part, :] -= one

    def rhs_place(chunk, block, piece):
        return rhs.at[chunk, block, pl.ds(piece * tall, tall)]

    def rhs_pass(chunk, step, pieces=range(SOURCE_PIECES)):
        pass_on(chunk, step, pieces, rhs_place, rhs_send, rhs_recv)

    def rhs_product(chunks, step, *quarter):
        if step == 0:
            accumulate(inverse_v, chunks, panel, rhs, "set", *quarter)
        else:
            for _, block, exists, _ in ways(step):
                @pl.when(exists)
                def _(block=block):
                    accumulate(inverse_v, chunks, block, rhs, "add", *quarter)

    def near_place(chunk, block, piece):
        return previous.at[chunk, block, pl.ds(piece * short, short)]

    def previous_pass(chunk, step):
        if step == 0:
            for piece in range(NEAR[chunk]):
                here = near_place(chunk, panel, piece)
                to_zone(chunk, panel, piece, here).wait_recv()
                if panels > 1:
                    for way, _, _, onward in ways(0):
                        @pl.when(onward)
                        def _(way=way, piece=piece, here=here):
                            line(way, chunk, 0, piece, here, near_send, near_recv).start()
        else:
            pass_on(chunk, step, range(NEAR[chunk]), near_place, near_send, near_recv)

    def previous_product(step):
        def one(block):
            for chunk in range(CHUNKS):
                for piece in range(NEAR[chunk], PIECES):
                    to_zone(chunk, block, piece, near_place(chunk, block, piece)).wait_recv()
            accumulate(coupling_v, (0, 1), block, previous, "subtract")

        if step == 0:
            one(panel)
        else:
            for _, block, exists, _ in ways(step):
                @pl.when(exists)
                def _(block=block):
                    one(block)

    def own(chunk, piece):
        return mine.at[chunk, pl.ds(piece * short, short)]

    def far_place(chunk, block, piece):
        return passing.at[block, pl.ds(piece * short, short)]

    def finish(chunk):
        @pl.when(has_next)
        def _():
            mine[chunk] = total[chunk].astype(mine.dtype)
            near = NEAR[chunk]
            for piece in range(near):
                to_zone(chunk, panel, piece, own(chunk, piece)).start()

            def hand_over(block, piece):
                from_ref = own(chunk, near + piece) if step == 0 else far_place(chunk, block, piece)
                to_zone(chunk, block, near + piece, from_ref).start()

            if near < PIECES:
                for step in range(panels):
                    pass_on(
                        chunk, step, range(PIECES - near), far_place, far_send, far_recv,
                        (lambda piece: own(chunk, near + piece)) if step == 0 else None, hand_over,
                    )

    def give(chunk):
        out[0, :, columns_of(chunk)] = total[chunk].astype(out.dtype)

    last, quarters = panels - 1, min(4, rows // 128)
    is_first = jnp.logical_not(has_before)

    def in_first(action):
        pl.when(is_first)(action)

    def in_later(action):
        pl.when(has_before)(action)

    rhs_pass(0, 0)
    for step in range(1, panels):
        rhs_pass(0, step)
        if step == 1:
            rhs_pass(1, 0)
            load_inverse.wait()
        if step == last:
            @in_first
            def _(step=step):
                rhs_product((0,), step - 1)
                rhs_product((0,), step)
                finish(0)
        if step > 1:
            rhs_pass(1, step - 1)

        @in_first
        def _(step=step):
            if step < last:
                rhs_product((0,), step - 1)
            rhs_product((1,), step - 1)

        if step == last:
            @in_later
            def _():
                previous_pass(0, 0)

        @in_later
        def _(step=step):
            rhs_product((0, 1), step - 1)

    if panels == 1:
        rhs_pass(1, 0)
        load_inverse.wait()

        @in_first
        def _():
            rhs_product((0,), 0)
            finish(0)

        @in_later
        def _():
            previous_pass(0, 0)
        @in_first
        def _():
            rhs_product((1,), 0)
    else:
        each = SOURCE_PIECES // quarters
        for part in range(quarters):
            rhs_pass(1, last, range(part * each, (part + 1) * each))

            @in_first
            def _(part=part):
                rhs_product((1,), last, part, quarters)

    @in_first
    def _():
        load_coupling.wait()

    @in_later
    def _():
        if last >= 1:
            previous_pass(0, 1)
        rhs_product((0, 1), last)
        load_coupling.wait()
        previous_pass(1, 0)
        for step in range(2, panels):
            previous_pass(0, step)
            previous_pass(1, step - 1)
            if step == 2:
                previous_product(0)
            previous_product(step - 1)
        if last <= 1:
            previous_product(0)
        if last >= 1:
            previous_pass(1, last)
            previous_product(last)
        finish(0)

    finish(1)
    for chunk in range(CHUNKS):
        give(chunk)

    for chunk in range(CHUNKS):
        sent(chunk, SOURCE_PIECES, rhs_place, rhs_send, rhs_recv)

        @pl.when(has_before)
        def _(chunk=chunk):
            sent(chunk, NEAR[chunk], near_place, near_send, near_recv)

        @pl.when(has_next)
        def _(chunk=chunk):
            sent(chunk, PIECES - NEAR[chunk], far_place, far_send, far_recv)
            for piece in range(NEAR[chunk]):
                to_zone(chunk, panel, piece, own(chunk, piece)).wait_send()
            for block in range(panels):
                for piece in range(NEAR[chunk], PIECES):
                    to_zone(chunk, block, piece, own(chunk, piece)).wait_send()


def solution(mesh):
    panels, zones = mesh.shape["panel"], mesh.shape["zone"]

    def local(source, inverse, coupling):
        _, rows, cols = source.shape
        unknowns = inverse.shape[2]
        width = cols // CHUNKS
        steps = max(panels - 1, 1)
        dma = pltpu.SemaphoreType.DMA
        anywhere = pl.BlockSpec(memory_space=pltpu.HBM)
        return pl.pallas_call(
            functools.partial(kernel, panels, zones),
            out_shape=jax.ShapeDtypeStruct(source.shape, jnp.bfloat16),
            in_specs=[anywhere] * 3,
            out_specs=pl.BlockSpec(memory_space=pltpu.VMEM),
            scratch_shapes=[
                pltpu.VMEM((rows, unknowns), jnp.bfloat16),
                pltpu.VMEM((rows, unknowns), jnp.bfloat16),
                pltpu.VMEM((CHUNKS, panels, rows, width), jnp.bfloat16),
                pltpu.VMEM((CHUNKS, panels, rows, width), jnp.bfloat16),
                pltpu.VMEM((panels, rows // PIECES * FAR, width), jnp.bfloat16),
                pltpu.VMEM((CHUNKS, rows, width), jnp.float32),
                pltpu.VMEM((CHUNKS, rows, width), jnp.bfloat16),
                dma((CHUNKS + 2,)),
                dma((CHUNKS, 2, steps, SOURCE_PIECES)), dma((CHUNKS, 2, steps, SOURCE_PIECES)),
                dma((CHUNKS, 2, steps, PIECES)), dma((CHUNKS, 2, steps, PIECES)),
                dma((CHUNKS, 2, steps, FAR)), dma((CHUNKS, 2, steps, FAR)),
                dma((CHUNKS, panels, PIECES)), dma((CHUNKS, panels, PIECES)),
            ],
            compiler_params=pltpu.CompilerParams(
                collective_id=0, has_side_effects=True, vmem_limit_bytes=48 * 2**20
            ),
            cost_estimate=pl.CostEstimate(
                flops=4 * rows * unknowns * cols, bytes_accessed=4 * rows * unknowns, transcendentals=0
            ),
        )(source, inverse, coupling)

    return jax.shard_map(
        local,
        mesh=mesh,
        in_specs=(
            P(("parts", "zone"), "panel", "rhs"),
            P(("parts", "zone"), "panel", None),
            P(("parts", "zone"), "panel", None),
        ),
        out_specs=P(("parts", "zone"), "panel", "rhs"),
        check_vma=False,
    )
```

```python
import functools

import jax
import jax.numpy as jnp
from jax import lax
from jax.experimental import pallas as pl
from jax.experimental.pallas import tpu as pltpu
from jax.sharding import PartitionSpec as P

MESH = pl.DeviceIdType.MESH
RIGHT, LEFT = 0, 1
CHUNKS = 2
SOURCE_PIECES = 4
PIECES = 8
NEAR = (8, 2)
FAR = max(PIECES - near for near in NEAR)


def kernel(
    panels, zones, source, inverse, coupling, out,
    inverse_v, coupling_v, rhs, previous, passing, total, mine,
    local_sem, rhs_send, rhs_recv, near_send, near_recv, far_send, far_recv, zone_send, zone_recv,
):
    panel, zone = lax.axis_index("panel"), lax.axis_index("zone")
    _, rows, width = mine.shape
    tall, short = rows // SOURCE_PIECES, rows // PIECES
    tile = min(rows, 1024)
    has_right, has_left = panel < panels - 1, panel > 0
    has_next, has_before = zone < zones - 1, zone > 0

    def columns_of(chunk):
        return pl.ds(chunk * width, width)

    load_rhs = [
        pltpu.make_async_copy(source.at[0, :, columns_of(c)], rhs.at[c, panel], local_sem.at[c])
        for c in range(CHUNKS)
    ]
    load_inverse = pltpu.make_async_copy(inverse.at[0], inverse_v, local_sem.at[CHUNKS])
    load_coupling = pltpu.make_async_copy(coupling.at[0], coupling_v, local_sem.at[CHUNKS + 1])
    for load in load_rhs:
        load.start()

    barrier = pltpu.get_barrier_semaphore()
    count = jnp.int32(0)
    for exists, axis, other in (
        (has_right, "panel", panel + 1),
        (has_left, "panel", panel - 1),
        (has_next, "zone", zone + 1),
        (has_before, "zone", zone - 1),
    ):
        @pl.when(exists)
        def _(axis=axis, other=other):
            pl.semaphore_signal(barrier, inc=1, device_id={axis: other}, device_id_type=MESH)

        count = count + exists.astype(jnp.int32)
    for load in load_rhs:
        load.wait()
    load_inverse.start()
    load_coupling.start()
    pl.semaphore_wait(barrier, count)

    def line(way, chunk, step, piece, here, send, recv, start=None):
        neighbour = panel + 1 if way == RIGHT else panel - 1
        return pltpu.make_async_remote_copy(
            src_ref=here if start is None else start, dst_ref=here,
            send_sem=send.at[chunk, way, step, piece], recv_sem=recv.at[chunk, way, step, piece],
            device_id={"panel": neighbour}, device_id_type=MESH,
        )

    def to_zone(chunk, block, piece, from_ref):
        return pltpu.make_async_remote_copy(
            src_ref=from_ref, dst_ref=previous.at[chunk, block, pl.ds(piece * short, short)],
            send_sem=zone_send.at[chunk, block, piece], recv_sem=zone_recv.at[chunk, block, piece],
            device_id={"zone": zone + 1}, device_id_type=MESH,
        )

    def ways(step):
        return (
            (RIGHT, panel - step, panel - step >= 0, has_right),
            (LEFT, panel + step, panel + step < panels, has_left),
        )

    def pass_on(chunk, step, pieces, place, send, recv, own=None, after=None):
        for piece in pieces:
            for way, block, exists, onward in ways(step):
                @pl.when(exists)
                def _(piece=piece, way=way, block=block, onward=onward):
                    here = place(chunk, block, piece)
                    if step > 0:
                        line(way, chunk, step - 1, piece, here, send, recv).wait_recv()
                    if step < panels - 1:
                        @pl.when(onward)
                        def _():
                            start = own(piece) if own is not None else None
                            line(way, chunk, step, piece, here, send, recv, start).start()
                    if step > 0 and after is not None:
                        after(block, piece)
            if step == 0 and after is not None:
                after(panel, piece)

    def sent(chunk, pieces, place, send, recv):
        for step in range(panels - 1):
            for piece in range(pieces):
                for way, block, exists, onward in ways(step):
                    @pl.when(jnp.logical_and(exists, onward))
                    def _(step=step, piece=piece, way=way, block=block):
                        line(way, chunk, step, piece, place(chunk, block, piece), send, recv).wait_send()

    def accumulate(matrix, chunks, block, vectors, kind, part_of=0, parts=1):
        depth = rows // parts
        columns = pl.ds(pl.multiple_of(block * rows + part_of * depth, depth), depth)
        inside = pl.ds(part_of * depth, depth)

        @pl.loop(0, rows // tile)
        def _(i):
            part = pl.ds(pl.multiple_of(i * tile, tile), tile)
            wide = jnp.concatenate([vectors[c, block, inside] for c in chunks], axis=1)
            product = jnp.dot(matrix[part, columns], wide, preferred_element_type=jnp.float32)
            for n, c in enumerate(chunks):
                one = product[:, n * width:(n + 1) * width]
                if kind == "set":
                    total[c, part, :] = one
                elif kind == "add":
                    total[c, part, :] += one
                else:
                    total[c, part, :] -= one

    def rhs_place(chunk, block, piece):
        return rhs.at[chunk, block, pl.ds(piece * tall, tall)]

    def rhs_pass(chunk, step, pieces=range(SOURCE_PIECES)):
        pass_on(chunk, step, pieces, rhs_place, rhs_send, rhs_recv)

    def rhs_product(chunks, step, *quarter):
        if step == 0:
            accumulate(inverse_v, chunks, panel, rhs, "set", *quarter)
        else:
            for _, block, exists, _ in ways(step):
                @pl.when(exists)
                def _(block=block):
                    accumulate(inverse_v, chunks, block, rhs, "add", *quarter)

    def near_place(chunk, block, piece):
        return previous.at[chunk, block, pl.ds(piece * short, short)]

    def previous_pass(chunk, step):
        if step == 0:
            for piece in range(NEAR[chunk]):
                here = near_place(chunk, panel, piece)
                to_zone(chunk, panel, piece, here).wait_recv()
                if panels > 1:
                    for way, _, _, onward in ways(0):
                        @pl.when(onward)
                        def _(way=way, piece=piece, here=here):
                            line(way, chunk, 0, piece, here, near_send, near_recv).start()
        else:
            pass_on(chunk, step, range(NEAR[chunk]), near_place, near_send, near_recv)

    def previous_product(step):
        def one(block):
            for chunk in range(CHUNKS):
                for piece in range(NEAR[chunk], PIECES):
                    to_zone(chunk, block, piece, near_place(chunk, block, piece)).wait_recv()
            accumulate(coupling_v, (0, 1), block, previous, "subtract")

        if step == 0:
            one(panel)
        else:
            for _, block, exists, _ in ways(step):
                @pl.when(exists)
                def _(block=block):
                    one(block)

    def own(chunk, piece):
        return mine.at[chunk, pl.ds(piece * short, short)]

    def far_place(chunk, block, piece):
        return passing.at[block, pl.ds(piece * short, short)]

    def finish(chunk):
        @pl.when(has_next)
        def _():
            mine[chunk] = total[chunk].astype(mine.dtype)
            near = NEAR[chunk]
            for piece in range(near):
                to_zone(chunk, panel, piece, own(chunk, piece)).start()

            def hand_over(block, piece):
                from_ref = own(chunk, near + piece) if step == 0 else far_place(chunk, block, piece)
                to_zone(chunk, block, near + piece, from_ref).start()

            if near < PIECES:
                for step in range(panels):
                    pass_on(
                        chunk, step, range(PIECES - near), far_place, far_send, far_recv,
                        (lambda piece: own(chunk, near + piece)) if step == 0 else None, hand_over,
                    )

    def give(chunk):
        out[0, :, columns_of(chunk)] = total[chunk].astype(out.dtype)

    last, quarters = panels - 1, min(4, rows // 128)
    is_first = jnp.logical_not(has_before)

    def in_first(action):
        pl.when(is_first)(action)

    def in_later(action):
        pl.when(has_before)(action)

    rhs_pass(0, 0)
    for step in range(1, panels):
        rhs_pass(0, step)
        if step == 1:
            rhs_pass(1, 0)
            load_inverse.wait()
        if step == last:
            @in_first
            def _(step=step):
                rhs_product((0,), step - 1)
                rhs_product((0,), step)
                finish(0)
        if step > 1:
            rhs_pass(1, step - 1)

        @in_first
        def _(step=step):
            if step < last:
                rhs_product((0,), step - 1)
            rhs_product((1,), step - 1)

        if step == last:
            @in_later
            def _():
                previous_pass(0, 0)

        @in_later
        def _(step=step):
            rhs_product((0, 1), step - 1)

    if panels == 1:
        rhs_pass(1, 0)
        load_inverse.wait()

        @in_first
        def _():
            rhs_product((0,), 0)
            finish(0)

        @in_later
        def _():
            previous_pass(0, 0)
        @in_first
        def _():
            rhs_product((1,), 0)
    else:
        each = SOURCE_PIECES // quarters
        for part in range(quarters):
            rhs_pass(1, last, range(part * each, (part + 1) * each))

            @in_first
            def _(part=part):
                rhs_product((1,), last, part, quarters)

    @in_first
    def _():
        load_coupling.wait()

    @in_later
    def _():
        if last >= 1:
            previous_pass(0, 1)
        rhs_product((0, 1), last)
        load_coupling.wait()
        previous_pass(1, 0)
        for step in range(2, panels):
            previous_pass(0, step)
            previous_pass(1, step - 1)
            if step == 2:
                previous_product(0)
            previous_product(step - 1)
        if last <= 1:
            previous_product(0)
        if last >= 1:
            previous_pass(1, last)
            previous_product(last)
        finish(0)

    finish(1)
    for chunk in range(CHUNKS):
        give(chunk)

    for chunk in range(CHUNKS):
        sent(chunk, SOURCE_PIECES, rhs_place, rhs_send, rhs_recv)

        @pl.when(has_before)
        def _(chunk=chunk):
            sent(chunk, NEAR[chunk], near_place, near_send, near_recv)

        @pl.when(has_next)
        def _(chunk=chunk):
            sent(chunk, PIECES - NEAR[chunk], far_place, far_send, far_recv)
            for piece in range(NEAR[chunk]):
                to_zone(chunk, panel, piece, own(chunk, piece)).wait_send()
            for block in range(panels):
                for piece in range(NEAR[chunk], PIECES):
                    to_zone(chunk, block, piece, own(chunk, piece)).wait_send()


def solution(mesh):
    panels, zones = mesh.shape["panel"], mesh.shape["zone"]

    def local(source, inverse, coupling):
        _, rows, cols = source.shape
        unknowns = inverse.shape[2]
        width = cols // CHUNKS
        steps = max(panels - 1, 1)
        dma = pltpu.SemaphoreType.DMA
        anywhere = pl.BlockSpec(memory_space=pltpu.HBM)
        return pl.pallas_call(
            functools.partial(kernel, panels, zones),
            out_shape=jax.ShapeDtypeStruct(source.shape, jnp.bfloat16),
            in_specs=[anywhere] * 3,
            out_specs=pl.BlockSpec(memory_space=pltpu.VMEM),
            scratch_shapes=[
                pltpu.VMEM((rows, unknowns), jnp.bfloat16),
                pltpu.VMEM((rows, unknowns), jnp.bfloat16),
                pltpu.VMEM((CHUNKS, panels, rows, width), jnp.bfloat16),
                pltpu.VMEM((CHUNKS, panels, rows, width), jnp.bfloat16),
                pltpu.VMEM((panels, rows // PIECES * FAR, width), jnp.bfloat16),
                pltpu.VMEM((CHUNKS, rows, width), jnp.float32),
                pltpu.VMEM((CHUNKS, rows, width), jnp.bfloat16),
                dma((CHUNKS + 2,)),
                dma((CHUNKS, 2, steps, SOURCE_PIECES)), dma((CHUNKS, 2, steps, SOURCE_PIECES)),
                dma((CHUNKS, 2, steps, PIECES)), dma((CHUNKS, 2, steps, PIECES)),
                dma((CHUNKS, 2, steps, FAR)), dma((CHUNKS, 2, steps, FAR)),
                dma((CHUNKS, panels, PIECES)), dma((CHUNKS, panels, PIECES)),
            ],
            compiler_params=pltpu.CompilerParams(
                collective_id=0, has_side_effects=True, vmem_limit_bytes=48 * 2**20
            ),
            cost_estimate=pl.CostEstimate(
                flops=4 * rows * unknowns * cols, bytes_accessed=4 * rows * unknowns, transcendentals=0
            ),
        )(source, inverse, coupling)

    return jax.shard_map(
        local,
        mesh=mesh,
        in_specs=(
            P(("parts", "zone"), "panel", "rhs"),
            P(("parts", "zone"), "panel", None),
            P(("parts", "zone"), "panel", None),
        ),
        out_specs=P(("parts", "zone"), "panel", "rhs"),
        check_vma=False,
    )
```
